32 devices in a mesh: groups: 2 (over y), space: 16 (over z, x, core).
Axes of the slice: x: 2, y: 2, z: 4, core: 2. Of those that a mesh axis runs over, the one named last changes fastest.
Arguments:
- density_band: bfloat16 [128, 9, 128, 128], P(('groups', 'space')), parts along dimension 0, may hold values from -0.009765625 to 0.009765625
- basis_values: bfloat16 [384, 5, 128, 128], P(('groups', 'space')), parts along dimension 0, may hold values from -6 to 6
- basis_grad: bfloat16 [3, 384, 5, 128, 128], P(None, ('groups', 'space')), parts along dimension 1, may hold values from -12 to 12
- quad_weights: float32 [384, 128], P(('groups', 'space')), parts along dimension 0, may hold values from 0.02 to 0.2
- significant_block_list: int32 [384, 5], P(('groups', 'space')), parts along dimension 0, may hold values from 0 to 63, as said below
- live_counts: int32 [384], P(('groups', 'space')), parts along dimension 0, may hold values from 1 to 5, as said below
- adjacency: int32 [384, 4], P(('groups', 'space')), parts along dimension 0, may hold values from 0 to 191
- atom_map: int32 [32, 512], P(('groups', 'space')), parts along dimension 0, may hold values from 0 to 46, never falling along the last dimension, each value on 1 to 24 neighbouring positions
- emb_scale: float32 [256], replicated, may hold values from -8 to 8
- emb_shift: float32 [256], replicated, may hold values from -3 to 3
- w_one: float32 [256, 256], replicated, may hold values from -0.375 to 0.375
- w_two: float32 [256, 256], replicated, may hold values from -0.375 to 0.375
- w_nonlocal: float32 [256, 256], replicated, may hold values from -1 to 1
- w_out: float32 [256], replicated, may hold values from -0.375 to 0.375
Outputs:
- potential_band_matrix: float32 [128, 9, 128, 128], P(('groups', 'space')), parts along dimension 0
- forces: float32 [3, 1504], P(None, ('groups', 'space')), parts along dimension 1
The draws below stay inside these ranges and needn't reach their ends.
There are 2 independent parts, one for each index of `groups`. The reference program is written for one: setup_inputs(seed, part) draws one part's arguments, and reference() takes and returns one part's arrays. A program takes and returns all parts, laid end to end along the dimension named above; an argument that names none is the same for every part. Nothing has to cross between parts.
Inputs may be any that keep to these rules, and one draw needn't show every extreme that they name: `significant_block_list`: each row's 5 block ids are distinct and consecutive in some order, and for batch b lie within blocks (b // 12) * 4 - 4 to (b // 12) * 4 + 7. `live_counts`: the first batch of every 12 has all 5 slots live.
All inputs are finite; a program needn't handle non-finite values.
Results may differ from the reference program's by a relative error of at most 0.0023.
Values may be sent and summed in bfloat16 or wider, within the bound.
A program may use at most 128 MiB of HBM per device.

```python
import math
import jax
import jax.numpy as jnp
import numpy as np
from jax import lax

BLK = 128
PTS = 128
C = 256
K = 5
H = 4
NADJ = 4
ATOM_DEV = 47
ATOM_MOST = 24
NBLK_DEV = 4
BATCH_DEV = 12
NB = 64
NBATCH = 192
ATOMS = 752
FUNC_DEV = 512
N_SPACE = 16


def draw_significant_block_list(key, part):
    key = jax.random.fold_in(key, 11)
    key_start, key_order = jax.random.split(key)
    batch_ids = jnp.arange(NBATCH, dtype=jnp.int32)
    device_ids = batch_ids // BATCH_DEV
    lowest = device_ids * NBLK_DEV - H
    spread = NBLK_DEV + 2 * H - K + 1
    window_start = lowest + jax.random.randint(key_start, (NBATCH,), 0, spread, dtype=jnp.int32)
    window_start = jnp.clip(window_start, 0, NB - K)
    window_start = window_start.at[0].set(0).at[NBATCH - 1].set(NB - K)
    scores = jax.random.randint(key_order, (NBATCH, K), 0, 1 << 20, dtype=jnp.int32) * K + jnp.arange(K, dtype=jnp.int32)[None, :]
    ordering = jnp.argsort(scores, axis=1).astype(jnp.int32)
    return (window_start[:, None] + ordering).astype(jnp.int32)


def draw_live_counts(key, part):
    key = jax.random.fold_in(key, 23)
    counted = jax.random.randint(key, (NBATCH,), 1, K + 1, dtype=jnp.int32)
    leading = jnp.arange(NBATCH, dtype=jnp.int32) % BATCH_DEV == 0
    return jnp.where(leading, K, counted).astype(jnp.int32)


def set_ends(array, key, least, high):
    shape = array.shape
    index_at = [jax.random.randint(jax.random.fold_in(key, axis), (), 0, shape[axis]) for axis in range(len(shape))]
    array = array.at[tuple(index_at)].set(least)
    longest = shape.index(max(shape))
    index_at[longest] = (index_at[longest] + 1) % shape[longest]
    return array.at[tuple(index_at)].set(high)


def block_scale(stream_key, dims, pieces, low, top_value):
    loudness, own = 1.0, jax.random.fold_in(stream_key, 6)
    for dim, parts in pieces:
        steps = jnp.exp(jax.random.uniform(jax.random.fold_in(own, dim), (parts,), jnp.float32, low / len(pieces), top_value / len(pieces)))
        loudness = loudness * jnp.repeat(steps, dims[dim] // parts).reshape([-1 if axis == dim else 1 for axis in range(len(dims))])
    return loudness


def profile(amount, total, reach, skew):
    loads = [(1 << 20) // math.isqrt(grade ** skew) + 1 for grade in range(2, amount + 1)]
    spare, counts = total - reach - (amount - 1), [1] * (amount - 1)
    while spare > 0:
        candidates = [i for i in range(amount - 1) if counts[i] < reach]
        whole, remaining = sum([loads[i] for i in candidates]), spare
        for i in candidates:
            extra = min(reach - counts[i], max(1, remaining * loads[i] // whole), spare)
            counts[i] = counts[i] + extra
            spare = spare - extra
    return np.array([reach] + counts)


def ragged(stream_key, amount, total, reach, skew):
    if amount == 2:
        one = jax.random.randint(stream_key, (), max(1, total - reach), min(reach, total - 1) + 1)
        return jnp.stack([one, total - one])
    sizes = jnp.asarray(profile(amount, total, reach, skew), jnp.int32)
    pairs = (amount - 1) // 2
    giver, receiver = sizes[1:1 + 2 * pairs:2], sizes[2:2 + 2 * pairs:2]
    margin = jnp.minimum(giver - 1, reach - receiver)
    moved = jax.random.randint(jax.random.fold_in(stream_key, 1), (pairs,), 0, 1 << 20) % (margin + 1)
    sizes = sizes.at[1:1 + 2 * pairs:2].set(giver - moved).at[2:2 + 2 * pairs:2].set(receiver + moved)
    return sizes[jax.random.permutation(jax.random.fold_in(stream_key, 2), amount)]


def normal_values(stream_key, extent, scale, most, cuts=(), kind=jnp.bfloat16):
    result = jax.random.normal(stream_key, extent, jnp.float32) * scale
    if len(cuts) > 0:
        result = block_scale(stream_key, extent, cuts, -0.22, 0.18) * result
    return jnp.clip(result, min=-most, max=most).astype(kind)


def setup_inputs(seed: int = 0, part: int = 0) -> dict:
    seeds = jax.random.split(jax.random.key(seed), 15)
    own_keys = jax.random.split(jax.random.fold_in(seeds[14], part), 15)
    return {
        "density_band": normal_values(own_keys[0], (NB, 2 * H + 1, BLK, BLK), (1.0 / (K * BLK)), 0.009765625, ((0, 16),)),
        "basis_values": normal_values(own_keys[1], (NBATCH, K, BLK, PTS), 1.0, 6.0, ((0, 16),)),
        "basis_grad": normal_values(own_keys[2], (3, NBATCH, K, BLK, PTS), 2.0, 12.0, ((1, 16),)),
        "quad_weights": jnp.clip(jnp.exp(math.log(0.2) - 2.3025851 * jax.random.uniform(own_keys[3], (NBATCH, PTS), jnp.float32) ** block_scale(own_keys[3], (NBATCH, PTS), ((0, 16),), -0.2, 0.2)), 0.02, 0.2),
        "significant_block_list": draw_significant_block_list(jax.random.fold_in(jax.random.fold_in(seeds[14], part), 71), part),
        "live_counts": draw_live_counts(jax.random.fold_in(jax.random.fold_in(seeds[14], part), 71), part),
        "adjacency": set_ends(jax.random.randint(own_keys[6], (NBATCH, NADJ), 0, NBATCH), jax.random.fold_in(own_keys[6], 1), 0, NBATCH - 1).astype(jnp.int32),
        "atom_map": jax.vmap(lambda own: jnp.searchsorted(jnp.cumsum(ragged(own, ATOM_DEV, FUNC_DEV, ATOM_MOST, 1)), jnp.arange(FUNC_DEV), side="right"))(jax.random.split(own_keys[7], N_SPACE)).reshape((N_SPACE, FUNC_DEV)).astype(jnp.int32),
        "emb_scale": normal_values(seeds[8], (C,), 1.5, 8.0, (), jnp.float32),
        "emb_shift": normal_values(seeds[9], (C,), 0.5, 3.0, (), jnp.float32),
        "w_one": normal_values(seeds[10], (C, C), C ** -0.5, 0.375, (), jnp.float32),
        "w_two": normal_values(seeds[11], (C, C), C ** -0.5, 0.375, (), jnp.float32),
        "w_nonlocal": normal_values(seeds[12], (C, C), (C // 8) ** -0.5, 1.0, (), jnp.float32),
        "w_out": normal_values(seeds[13], (C,), C ** -0.5, 0.375, (), jnp.float32),
    }


PRECISE = lax.Precision.HIGHEST

def front_layers(density_in, weights_in, emb_scale, emb_shift, w_one):
    embedded = jnp.tanh(density_in[..., None] * emb_scale + emb_shift)
    hidden_one = jax.nn.silu(jnp.matmul(embedded, w_one, precision=PRECISE))
    coarse = jnp.einsum('bp,bpc->bc', weights_in * density_in, hidden_one, precision=PRECISE)
    return (hidden_one, coarse)

def back_layers(density_in, weights_in, hidden_one, near_mean, w_two, w_nonlocal, w_out):
    combined = jnp.matmul(hidden_one, w_two, precision=PRECISE) + jnp.matmul(near_mean, w_nonlocal, precision=PRECISE)[:, None, :]
    local_energy = jnp.matmul(jax.nn.silu(combined), w_out, precision=PRECISE)
    return jnp.sum(weights_in * density_in * local_energy)

def reference(density_band, basis_values, basis_grad, quad_weights, significant_block_list, live_counts, adjacency, atom_map, emb_scale, emb_shift, w_one, w_two, w_nonlocal, w_out):
    live_slots = jnp.arange(K).astype(jnp.int32)[None, :] < live_counts[:, None]
    masked_values = basis_values * live_slots[:, :, None, None].astype(jnp.bfloat16)
    live_fraction = live_slots.astype(jnp.float32)

    def project(slot_row_table, values):
        block_offsets = (slot_row_table[None, :] - slot_row_table[:, None] + H).astype(jnp.int32)
        basis_blocks = density_band[slot_row_table[:, None], block_offsets].astype(jnp.float32)
        return jnp.einsum('kjfh,jhg->kfg', basis_blocks, values.astype(jnp.float32), precision=PRECISE)

    def density_pass(inputs):
        projected = project(inputs[0], inputs[1])
        return lax.optimization_barrier(jnp.sum(inputs[1].astype(jnp.float32) * projected, axis=(0, 1)))
    density = lax.map(density_pass, (significant_block_list, masked_values))
    group_count = NBATCH // BATCH_DEV
    density_groups = density.reshape(group_count, BATCH_DEV, PTS)
    weight_groups = quad_weights.reshape(group_count, BATCH_DEV, PTS)

    def coarse_pass(inputs):
        return front_layers(inputs[0], inputs[1], emb_scale, emb_shift, w_one)[1]
    coarse = lax.map(coarse_pass, (density_groups, weight_groups)).reshape(NBATCH, C)
    near_mean = lax.optimization_barrier(jnp.mean(coarse[adjacency], axis=1))
    near_groups = near_mean.reshape(group_count, BATCH_DEV, C)

    def near_pass(inputs):
        density_in, weights_in, near_in = inputs
        hidden_one, ignored_value = front_layers(density_in, weights_in, emb_scale, emb_shift, w_one)
        return jax.grad(lambda near_arg: back_layers(density_in, weights_in, hidden_one, near_arg, w_two, w_nonlocal, w_out))(near_in)
    grad_near = lax.map(near_pass, (density_groups, weight_groups, near_groups)).reshape(NBATCH, C)
    grad_coarse = jnp.zeros((NBATCH, C), jnp.float32).at[adjacency.reshape(-1)].add(jnp.repeat(grad_near, NADJ, axis=0) / NADJ)
    coarse_groups = grad_coarse.reshape(group_count, BATCH_DEV, C)

    def potential_pass(inputs):
        density_in, weights_in, near_in, grad_in = inputs
        front_out, pull_front = jax.vjp(lambda arg: front_layers(arg, weights_in, emb_scale, emb_shift, w_one), density_in)
        grad_direct, grad_hidden = jax.grad(lambda arg, hid: back_layers(arg, weights_in, hid, near_in, w_two, w_nonlocal, w_out), argnums=(0, 1))(density_in, front_out[0])
        grad_front, = pull_front((grad_hidden, grad_in))
        return grad_direct + grad_front
    potential = lax.map(potential_pass, (density_groups, weight_groups, near_groups, coarse_groups)).reshape(NBATCH, PTS)
    weighted_terms = quad_weights * potential
    gradient_shifted = jnp.moveaxis(basis_grad, 1, 0)

    def accumulate_terms(carried_state_pair, inputs):
        potential_window_slice, force_window_slice = carried_state_pair
        slot_row_table, values, gradient, weighted_row, live_row = inputs
        projected = project(slot_row_table, values)
        scaled = lax.optimization_barrier((values.astype(jnp.float32) * weighted_row).astype(jnp.bfloat16))
        basis_blocks = jnp.einsum('kfg,jhg->kjfh', scaled.astype(jnp.float32), values.astype(jnp.float32), precision=PRECISE)
        block_offsets = (slot_row_table[None, :] - slot_row_table[:, None] + H).astype(jnp.int32)
        potential_window_slice = potential_window_slice.at[slot_row_table[:, None], block_offsets].add(basis_blocks)
        partial_value = -2.0 * jnp.einsum('ckfg,kfg->ckf', gradient.astype(jnp.float32), projected * weighted_row * live_row[:, None, None], precision=PRECISE)
        force_window_slice = force_window_slice.at[:, slot_row_table].add(partial_value)
        return ((potential_window_slice, force_window_slice), None)
    initial_carry = (jnp.zeros((NB, 2 * H + 1, BLK, BLK), jnp.float32), jnp.zeros((3, NB, BLK), jnp.float32))
    (potential_band_matrix, force_band_matrix), ignored_value = lax.scan(accumulate_terms, initial_carry, (significant_block_list, masked_values, gradient_shifted, weighted_terms, live_fraction))
    function_forces = force_band_matrix.reshape(3, N_SPACE, FUNC_DEV)
    onehot = (atom_map[:, :, None] == jnp.arange(ATOM_DEV).astype(jnp.int32)[None, None, :]).astype(jnp.float32)
    forces = jnp.einsum('cnf,nfa->cna', function_forces, onehot, precision=PRECISE).reshape(3, ATOMS)
    return (potential_band_matrix, forces)
```

```python
import functools

import jax
import jax.numpy as jnp
from jax import lax
from jax.experimental import pallas as pl
from jax.experimental.pallas import tpu as pltpu
from jax.sharding import PartitionSpec as P

ATOM_DEV = 47
PAD = 16
CHUNK = 4
F32, BF16 = jnp.float32, jnp.bfloat16
VMEM = pl.BlockSpec(memory_space=pltpu.VMEM)
SMEM = pl.BlockSpec(memory_space=pltpu.SMEM)
ANY = pl.BlockSpec(memory_space=pl.ANY)
LIMIT = 48 * 1024 * 1024
NN = (((1,), (0,)), ((), ()))
NT = (((1,), (1,)), ((), ()))


def split(value):
    high = value.astype(BF16)
    return high, (value - high.astype(F32)).astype(BF16)


def mm(left, right, dims):
    return lax.dot_general(left, right, dims, preferred_element_type=F32)


def mm3(left, right, dims):
    return mm(left[0], right[0], dims) + (
        mm(left[0], right[1], dims) + mm(left[1], right[0], dims)
    )


def exact(left, value, dims):
    first, rest = value.astype(BF16), None
    rest = value - first.astype(F32)
    second, third = split(rest)
    return mm(left, first, dims) + (mm(left, second, dims) + mm(left, third, dims))


def greet_neighbours(me, count):
    barrier = pltpu.get_barrier_semaphore()
    for step, there in ((-1, me > 0), (1, me < count - 1)):

        @pl.when(there)
        def _():
            pl.semaphore_signal(barrier, inc=1, device_id={"space": me + step}, device_id_type=pl.DeviceIdType.MESH)

    inside = (me > 0) & (me < count - 1)

    @pl.when(inside)
    def _():
        pl.semaphore_wait(barrier, 2)

    @pl.when(jnp.logical_not(inside))
    def _():
        pl.semaphore_wait(barrier, 1)


def swap_body(count, to_up, to_down, me, pairs_up, pairs_down, send_up, recv_up, send_down, recv_down):
    def made(pairs, step, send, recv):
        return [
            pltpu.make_async_remote_copy(
                src_ref=a, dst_ref=b, send_sem=send.at[i], recv_sem=recv.at[i],
                device_id={"space": me + step}, device_id_type=pl.DeviceIdType.MESH,
            )
            for i, (a, b) in enumerate(pairs)
        ]

    has_next, has_before = me < count - 1, me > 0

    @pl.when(has_next)
    def _():
        for copy in made(pairs_up, 1, send_up, recv_up):
            copy.start()

    @pl.when(has_before)
    def _():
        for copy in made(pairs_down, -1, send_down, recv_down):
            copy.start()

    @pl.when(has_next)
    def _():
        for copy in made(pairs_up, 1, send_up, recv_up):
            copy.wait_send()
        for copy in made(pairs_down, 1, send_down, recv_down):
            copy.wait_recv()

    @pl.when(has_before)
    def _():
        for copy in made(pairs_down, -1, send_down, recv_down):
            copy.wait_send()
        for copy in made(pairs_up, -1, send_up, recv_up):
            copy.wait_recv()


def halo_kernel(count, half, band, below, above, *sems):
    me = lax.axis_index("space")
    greet_neighbours(me, count)
    rows, width = band.shape[0], 2 * half + 1
    up = [(band.at[i, half - i : width], below.at[i, half - i : width]) for i in range(rows)]
    down = [(band.at[i, 0 : width - 1 - i], above.at[i, 0 : width - 1 - i]) for i in range(rows)]
    swap_body(count, None, None, me, up, down, *sems)


def halo_swap(band, half, count):
    like = jax.ShapeDtypeStruct(band.shape, band.dtype)
    return pl.pallas_call(
        functools.partial(halo_kernel, count, half),
        out_shape=(like, like),
        in_specs=[ANY],
        out_specs=(ANY, ANY),
        scratch_shapes=[pltpu.SemaphoreType.DMA((band.shape[0],))] * 4,
        compiler_params=pltpu.CompilerParams(collective_id=0, has_side_effects=True),
        name="density_rows",
    )(band)


def masked(values, live, stacked):
    slots, block = values.shape[1], values.shape[2]
    for k in range(slots):
        block_values = values[0, k]
        stacked[k * block : (k + 1) * block] = jnp.where(k < live, block_values, jnp.zeros_like(block_values))


def density_kernel(slots_ref, live_ref, band, below, above, values, density, projected, window, stacked, sems):
    b = pl.program_id(0)
    rows, width, block = band.shape[0], band.shape[1], band.shape[2]
    half = (width - 1) // 2
    slots = values.shape[1]
    first = lax.axis_index("space") * rows - half

    @pl.when(b == 0)
    def _():
        copies = [
            pltpu.make_async_copy(part, window.at[pl.ds(i * rows, rows)], sems.at[i])
            for i, part in enumerate((below, band, above))
        ]
        for copy in copies:
            copy.start()
        for copy in copies:
            copy.wait()

    live = live_ref[b]
    masked(values, live, stacked)
    ids = [slots_ref[b, k] - first for k in range(slots)]
    whole = stacked[...]
    total = jnp.zeros((1, values.shape[3]), F32)
    for k in range(slots):
        lhs = jnp.concatenate([window[ids[k], ids[j] - ids[k] + half] for j in range(slots)], axis=1)
        result = mm(lhs, whole, NN)
        result = jnp.where(k < live, result, jnp.zeros_like(result))
        projected[0, k] = result
        total = total + jnp.sum(result * stacked[k * block : (k + 1) * block].astype(F32), axis=0, keepdims=True)
    density[pl.ds(b, 1), :] = total


def density_call(slot_ids, live, band, below, above, values):
    batches, slots, block, points = values.shape
    rows, width = band.shape[:2]
    return pl.pallas_call(
        density_kernel,
        grid=(batches,),
        out_shape=(
            jax.ShapeDtypeStruct((batches, points), F32),
            jax.ShapeDtypeStruct(values.shape, F32),
        ),
        in_specs=[SMEM, SMEM, ANY, ANY, ANY, pl.BlockSpec((1, slots, block, points), lambda b: (b, 0, 0, 0))],
        out_specs=(
            pl.BlockSpec((batches, points), lambda b: (0, 0)),
            pl.BlockSpec((1, slots, block, points), lambda b: (b, 0, 0, 0)),
        ),
        scratch_shapes=[
            pltpu.VMEM((3 * rows, width, block, block), BF16),
            pltpu.VMEM((slots * block, points), BF16),
            pltpu.SemaphoreType.DMA((3,)),
        ],
        compiler_params=pltpu.CompilerParams(vmem_limit_bytes=LIMIT),
        name="density",
    )(slot_ids, live, band, below, above, values)


def network_kernel(
    count, density, weights, adjacency, emb_scale, emb_shift, w_one, w_two, w_nonlocal, w_out, out,
    hidden, slope, mixed, mixed_slope, table, coarse, gathered, parts, summed, s1, r1, s2, r2,
):
    me = lax.axis_index("space")
    barrier = pltpu.get_barrier_semaphore()

    def greet(i, carry):
        pl.semaphore_signal(
            barrier, inc=1, device_id={"space": lax.rem(me + i, count)}, device_id_type=pl.DeviceIdType.MESH
        )
        return carry

    lax.fori_loop(1, count, greet, 0)
    batches, points = density.shape
    channels = w_one.shape[0]
    span = CHUNK * points
    near_count = adjacency.shape[1]
    one_t, two_t = split(w_one[...].T), split(w_two[...].T)
    scale, shift, read = emb_scale[...], emb_shift[...], w_out[...]

    def row_of(ref, i):
        return jnp.concatenate([ref[i * CHUNK + j : i * CHUNK + j + 1, :] for j in range(CHUNK)], axis=1)

    def spread(row, i):
        wide = jnp.broadcast_to(row, (PAD, span))
        place = lax.broadcasted_iota(jnp.int32, (PAD, span), 0)
        lane = lax.broadcasted_iota(jnp.int32, (PAD, span), 1)
        return jnp.where(place == lane // points + i * CHUNK, wide, 0.0)

    steps = batches // CHUNK
    total = jnp.zeros((PAD, channels), F32)
    for i in range(steps):
        at = slice(i * span, (i + 1) * span)
        row = row_of(density, i)
        embedded = jnp.tanh(scale * row + shift)
        rising = (1.0 - embedded * embedded) * scale
        pre = mm3(one_t, split(embedded), NN)
        gate = 1.0 / (1.0 + jnp.exp(-pre))
        hid = pre * gate
        hidden[:, at] = hid
        slope[:, at] = mm3(one_t, split(rising), NN) * (gate * (1.0 + pre * (1.0 - gate)))
        total = total + mm3(split(spread(row_of(weights, i) * row, i)), split(hid), NT)
    coarse[...] = total
    gathered[me] = total

    pl.semaphore_wait(barrier, count - 1)

    def send_one(i, carry):
        peer = lax.rem(me + i, count)
        pltpu.make_async_remote_copy(
            src_ref=coarse, dst_ref=gathered.at[me], send_sem=s1, recv_sem=r1,
            device_id={"space": peer}, device_id_type=pl.DeviceIdType.MESH,
        ).start()
        return carry

    lax.fori_loop(1, count, send_one, 0)

    for i in range(steps):
        at = slice(i * span, (i + 1) * span)
        mixed[:, at] = mm3(two_t, split(hidden[:, at]), NN)
        mixed_slope[:, at] = mm3(two_t, split(slope[:, at]), NN)
    long = count * PAD
    column = lax.broadcasted_iota(jnp.int32, (128, long), 1)
    place = column & (PAD - 1)
    ids = jnp.where(place < batches, (column >> 4) * batches + place, -1)
    listed = jnp.concatenate([adjacency[...], jnp.full((128 - batches, near_count), -2, jnp.int32)], axis=0)
    hits = jnp.zeros((128, long), F32)
    for a in range(near_count):
        hits = hits + jnp.where(listed[:, a : a + 1] == ids, 1.0 / near_count, 0.0)
    table[...] = hits
    turned = hits.T.astype(BF16)
    far = split(w_nonlocal[...])
    far_t = split(w_nonlocal[...].T)

    both = gathered.at[pl.ds(0, count - 1)]
    pltpu.make_async_copy(both, both, r1).wait()
    near = exact(table[0:PAD, :].astype(BF16), gathered[...].reshape(long, channels), NN)
    near = jnp.concatenate([near, jnp.zeros((128 - PAD, channels), F32)], axis=0)
    offsets = mm3(far_t, split(near.T), NN)

    pulled = jnp.zeros((PAD, channels), F32)
    direct = []
    for i in range(steps):
        at = slice(i * span, (i + 1) * span)
        offset = jnp.concatenate(
            [
                jnp.broadcast_to(offsets[:, i * CHUNK + j : i * CHUNK + j + 1], (channels, points))
                for j in range(CHUNK)
            ],
            axis=1,
        )
        pre = mixed[:, at] + offset
        gate = 1.0 / (1.0 + jnp.exp(-pre))
        row_w = row_of(weights, i)
        row_wd = row_w * row_of(density, i)
        bent = gate * (1.0 + pre * (1.0 - gate)) * read
        pulled = pulled + mm3(split(spread(row_wd, i)), split(bent), NT)
        energy = jnp.sum(pre * gate * read, axis=0, keepdims=True)
        direct.append(row_w * energy + row_wd * jnp.sum(bent * mixed_slope[:, at], axis=0, keepdims=True))
    grad_near = mm3(split(pulled), far, NT)
    grad_near = jnp.concatenate([grad_near, jnp.zeros((128 - PAD, channels), F32)], axis=0)
    parts[...] = exact(turned, grad_near, NN).reshape(count, PAD, channels)
    summed[me] = parts[me]

    def send_two(i, carry):
        peer = lax.rem(me + i, count)
        pltpu.make_async_remote_copy(
            src_ref=parts.at[peer], dst_ref=summed.at[me], send_sem=s2, recv_sem=r2,
            device_id={"space": peer}, device_id_type=pl.DeviceIdType.MESH,
        ).start()
        return carry

    lax.fori_loop(1, count, send_two, 0)
    for i in range(steps):
        at = slice(i * span, (i + 1) * span)
        mixed[:, at] = hidden[:, at] + row_of(density, i) * slope[:, at]
    other = summed.at[pl.ds(0, count - 1)]
    pltpu.make_async_copy(other, other, r2).wait()
    grad_coarse = jnp.sum(summed[...], axis=0)
    grad_coarse = jnp.concatenate([grad_coarse, jnp.zeros((128 - PAD, channels), F32)], axis=0).T
    for i in range(steps):
        for j in range(CHUNK):
            b = i * CHUNK + j
            piece = mixed[:, b * points : (b + 1) * points] * grad_coarse[:, b : b + 1]
            row_w = weights[b : b + 1, :]
            value = direct[i][:, j * points : (j + 1) * points] + row_w * jnp.sum(piece, axis=0, keepdims=True)
            out[b : b + 1, :] = value * row_w
    pltpu.make_async_copy(both, both, s1).wait()
    pltpu.make_async_copy(other, other, s2).wait()


def network(density, weights, adjacency, emb_scale, emb_shift, w_one, w_two, w_nonlocal, w_out, count):
    batches, points = density.shape
    channels = w_one.shape[0]
    wide = pltpu.VMEM((channels, batches * points), F32)
    slots = pltpu.VMEM((count, PAD, channels), F32)
    return pl.pallas_call(
        functools.partial(network_kernel, count),
        out_shape=jax.ShapeDtypeStruct((batches, points), F32),
        in_specs=[VMEM] * 9,
        out_specs=VMEM,
        scratch_shapes=[wide] * 4
        + [pltpu.VMEM((128, count * PAD), F32), pltpu.VMEM((PAD, channels), F32), slots, slots, slots]
        + [pltpu.SemaphoreType.DMA] * 4,
        compiler_params=pltpu.CompilerParams(collective_id=1, has_side_effects=True, vmem_limit_bytes=LIMIT),
        name="network",
    )(density, weights, adjacency, emb_scale[:, None], emb_shift[:, None], w_one, w_two, w_nonlocal, w_out[:, None])


def terms_kernel(
    rows, slots_ref, live_ref, potential, values, grads, projected, own, below, above, force, acc, facc, stacked
):
    b = pl.program_id(0)
    slots, block = values.shape[1], values.shape[2]
    width = own.shape[1]
    half = (width - 1) // 2
    first = lax.axis_index("space") * rows - half

    @pl.when(b == 0)
    def _():
        acc[...] = jnp.zeros_like(acc)
        facc[...] = jnp.zeros_like(facc)

    live = live_ref[b]
    masked(values, live, stacked)
    ids = [slots_ref[b, k] - first for k in range(slots)]
    whole = stacked[...]
    row = potential[pl.ds(b, 1), :]
    ones = jnp.ones((8, block), BF16)
    for k in range(slots):
        scaled = (stacked[k * block : (k + 1) * block].astype(F32) * row).astype(BF16)
        result = mm(scaled, whole, NT)
        for j in range(slots):
            place = ids[k] * width + ids[j] - ids[k] + half
            acc[place] += result[:, j * block : (j + 1) * block]
        carried = projected[0, k] * row
        product = jnp.concatenate([grads[c, 0, k].astype(F32) * carried for c in range(3)], axis=0)
        high, low = split(product)
        facc[ids[k]] += -2.0 * (mm(ones, high, NT) + mm(ones, low, NT))

    @pl.when(b == pl.num_programs(0) - 1)
    def _():
        for i in range(rows):
            for o in range(width):
                below[i, o] = acc[i * width + o].astype(BF16)
                own[i, o] = acc[(rows + i) * width + o]
                above[i, o] = acc[(2 * rows + i) * width + o].astype(BF16)
        force[...] = facc[...]


def terms(slot_ids, live, potential, values, grads, projected, rows, width):
    batches, slots, block, points = values.shape
    four = lambda b: (0, 0, 0, 0)
    shape = (rows, width, block, block)
    return pl.pallas_call(
        functools.partial(terms_kernel, rows),
        grid=(batches,),
        out_shape=(
            jax.ShapeDtypeStruct(shape, F32),
            jax.ShapeDtypeStruct(shape, BF16),
            jax.ShapeDtypeStruct(shape, BF16),
            jax.ShapeDtypeStruct((3 * rows, 8, 3 * block), F32),
        ),
        in_specs=[
            SMEM,
            SMEM,
            pl.BlockSpec((batches, points), lambda b: (0, 0)),
            pl.BlockSpec((1, slots, block, points), lambda b: (b, 0, 0, 0)),
            pl.BlockSpec((3, 1, slots, block, points), lambda b: (0, b, 0, 0, 0)),
            pl.BlockSpec((1, slots, block, points), lambda b: (b, 0, 0, 0)),
        ],
        out_specs=(
            pl.BlockSpec(shape, four),
            pl.BlockSpec(shape, four),
            pl.BlockSpec(shape, four),
            pl.BlockSpec((3 * rows, 8, 3 * block), lambda b: (0, 0, 0)),
        ),
        scratch_shapes=[
            pltpu.VMEM((3 * rows * width, block, block), F32),
            pltpu.VMEM((3 * rows, 8, 3 * block), F32),
            pltpu.VMEM((slots * block, points), BF16),
        ],
        compiler_params=pltpu.CompilerParams(vmem_limit_bytes=LIMIT),
        name="terms",
    )(slot_ids, live, potential, values, grads, projected)


def return_kernel(count, half, below, above, force, from_above, from_below, force_above, force_below, *sems):
    me = lax.axis_index("space")
    greet_neighbours(me, count)
    rows, width = below.shape[0], 2 * half + 1
    down = [(below.at[i, half - i : width], from_above.at[i, half - i : width]) for i in range(rows)]
    up = [(above.at[i, 0 : width - 1 - i], from_below.at[i, 0 : width - 1 - i]) for i in range(rows)]
    down.append((force.at[0:rows], force_above))
    up.append((force.at[2 * rows : 3 * rows], force_below))
    swap_body(count, None, None, me, up, down, *sems)


def return_swap(below, above, force, half, count):
    like = jax.ShapeDtypeStruct(below.shape, below.dtype)
    rows = below.shape[0]
    small = jax.ShapeDtypeStruct((rows,) + force.shape[1:], force.dtype)
    return pl.pallas_call(
        functools.partial(return_kernel, count, half),
        out_shape=(like, like, small, small),
        in_specs=[ANY] * 3,
        out_specs=(ANY,) * 4,
        scratch_shapes=[pltpu.SemaphoreType.DMA((rows + 1,))] * 4,
        compiler_params=pltpu.CompilerParams(collective_id=2, has_side_effects=True),
        name="returned_rows",
    )(below, above, force)


def final_kernel(count, own, from_above, from_below, force, force_above, force_below, atoms, out, forces):
    i = pl.program_id(0)
    me = lax.axis_index("space")
    width = own.shape[1]
    half = (width - 1) // 2
    rows = force_above.shape[0]
    block = own.shape[2]
    for o in range(width):
        value = own[0, o]
        upper = from_above[0, o].astype(F32)
        lower = from_below[0, o].astype(F32)
        value = value + jnp.where((me < count - 1) & (o >= half - i), upper, jnp.zeros_like(upper))
        out[0, o] = value + jnp.where((me > 0) & (o <= width - 2 - i), lower, jnp.zeros_like(lower))

    @pl.when(i == pl.num_programs(0) - 1)
    def _():
        lines = []
        for c in range(3):
            pieces = []
            for r in range(rows):
                at = slice(c * block, (c + 1) * block)
                a, b = force_above[r, 0:1, at], force_below[r, 0:1, at]
                pieces.append(
                    force[rows + r, 0:1, at]
                    + jnp.where(me < count - 1, a, jnp.zeros_like(a))
                    + jnp.where(me > 0, b, jnp.zeros_like(b))
                )
            lines.append(jnp.concatenate(pieces, axis=1))
        lines = jnp.concatenate(lines + [jnp.zeros((5, rows * block), F32)], axis=0)
        named = atoms[...]
        hot = jnp.where(lax.broadcasted_iota(jnp.int32, (128, rows * block), 0) == named, 1.0, 0.0).astype(BF16)
        first, rest = lines.astype(BF16), None
        rest = lines - first.astype(F32)
        second, third = split(rest)
        result = mm(first, hot, NT) + (mm(second, hot, NT) + mm(third, hot, NT))
        forces[...] = result[0:3, 0:ATOM_DEV]


def final(own, from_above, from_below, force, force_above, force_below, atoms, count):
    rows, width, block, _ = own.shape
    row_spec = pl.BlockSpec((1, width, block, block), lambda i: (i, 0, 0, 0))
    full = lambda a: pl.BlockSpec(a.shape, lambda i: (0,) * a.ndim)
    return pl.pallas_call(
        functools.partial(final_kernel, count),
        grid=(rows,),
        out_shape=(jax.ShapeDtypeStruct(own.shape, F32), jax.ShapeDtypeStruct((3, ATOM_DEV), F32)),
        in_specs=[row_spec] * 3 + [full(force), full(force_above), full(force_below), full(atoms)],
        out_specs=(row_spec, pl.BlockSpec((3, ATOM_DEV), lambda i: (0, 0))),
        compiler_params=pltpu.CompilerParams(vmem_limit_bytes=LIMIT),
        name="final",
    )(own, from_above, from_below, force, force_above, force_below, atoms)


def per_device(
    density_band, basis_values, basis_grad, quad_weights, significant_block_list, live_counts,
    adjacency, atom_map, emb_scale, emb_shift, w_one, w_two, w_nonlocal, w_out,
):
    rows, width = density_band.shape[:2]
    half = (width - 1) // 2
    count = lax.axis_size("space")
    below, above = halo_swap(density_band, half, count)
    density, projected = density_call(
        significant_block_list, live_counts, density_band, below, above, basis_values
    )
    potential = network(
        density, quad_weights, adjacency, emb_scale, emb_shift, w_one, w_two, w_nonlocal, w_out, count
    )
    own, low, high, force = terms(
        significant_block_list, live_counts, potential, basis_values, basis_grad, projected, rows, width
    )
    from_above, from_below, force_above, force_below = return_swap(low, high, force, half, count)
    return final(own, from_above, from_below, force, force_above, force_below, atom_map, count)


def solution(mesh):
    both = ("groups", "space")
    placed = (
        P(both, None, None, None),
        P(both, None, None, None),
        P(None, both, None, None, None),
        P(both, None),
        P(both, None),
        P(both),
        P(both, None),
        P(both, None),
    ) + (P(),) * 6
    return jax.shard_map(
        per_device,
        mesh=mesh,
        in_specs=placed,
        out_specs=(P(both, None, None, None), P(None, both)),
        check_vma=False,
    )
```

```python
import functools

import jax
import jax.numpy as jnp
from jax import lax
from jax.experimental import pallas as pl
from jax.experimental.pallas import tpu as pltpu
from jax.sharding import PartitionSpec as P

ATOM_DEV = 47
PAD = 16
CHUNK = 4
F32, BF16 = jnp.float32, jnp.bfloat16
VMEM = pl.BlockSpec(memory_space=pltpu.VMEM)
SMEM = pl.BlockSpec(memory_space=pltpu.SMEM)
ANY = pl.BlockSpec(memory_space=pl.ANY)
LIMIT = 60 * 1024 * 1024
NN = (((1,), (0,)), ((), ()))
NT = (((1,), (1,)), ((), ()))


def split(value):
    high = value.astype(BF16)
    return high, (value - high.astype(F32)).astype(BF16)


def mm(left, right, dims):
    return lax.dot_general(left, right, dims, preferred_element_type=F32)


def mm3(left, right, dims):
    return mm(left[0], right[0], dims) + (
        mm(left[0], right[1], dims) + mm(left[1], right[0], dims)
    )


def exact(left, value, dims):
    first, rest = value.astype(BF16), None
    rest = value - first.astype(F32)
    second, third = split(rest)
    return mm(left, first, dims) + (mm(left, second, dims) + mm(left, third, dims))


def greet_neighbours(me, count):
    barrier = pltpu.get_barrier_semaphore()
    for step, there in ((-1, me > 0), (1, me < count - 1)):

        @pl.when(there)
        def _():
            pl.semaphore_signal(barrier, inc=1, device_id={"space": me + step}, device_id_type=pl.DeviceIdType.MESH)

    inside = (me > 0) & (me < count - 1)

    @pl.when(inside)
    def _():
        pl.semaphore_wait(barrier, 2)

    @pl.when(jnp.logical_not(inside))
    def _():
        pl.semaphore_wait(barrier, 1)


def swap_body(count, to_up, to_down, me, pairs_up, pairs_down, send_up, recv_up, send_down, recv_down):
    def made(pairs, step, send, recv):
        return [
            pltpu.make_async_remote_copy(
                src_ref=a, dst_ref=b, send_sem=send.at[i], recv_sem=recv.at[i],
                device_id={"space": me + step}, device_id_type=pl.DeviceIdType.MESH,
            )
            for i, (a, b) in enumerate(pairs)
        ]

    has_next, has_before = me < count - 1, me > 0

    @pl.when(has_next)
    def _():
        for copy in made(pairs_up, 1, send_up, recv_up):
            copy.start()

    @pl.when(has_before)
    def _():
        for copy in made(pairs_down, -1, send_down, recv_down):
            copy.start()

    @pl.when(has_next)
    def _():
        for copy in made(pairs_up, 1, send_up, recv_up):
            copy.wait_send()
        for copy in made(pairs_down, 1, send_down, recv_down):
            copy.wait_recv()

    @pl.when(has_before)
    def _():
        for copy in made(pairs_down, -1, send_down, recv_down):
            copy.wait_send()
        for copy in made(pairs_up, -1, send_up, recv_up):
            copy.wait_recv()


def halo_kernel(count, half, band, below, above, *sems):
    me = lax.axis_index("space")
    greet_neighbours(me, count)
    rows, width = band.shape[0], 2 * half + 1
    up = [(band.at[i, half - i : width], below.at[i, half - i : width]) for i in range(rows)]
    down = [(band.at[i, 0 : width - 1 - i], above.at[i, 0 : width - 1 - i]) for i in range(rows)]
    swap_body(count, None, None, me, up, down, *sems)


def halo_swap(band, half, count):
    like = jax.ShapeDtypeStruct(band.shape, band.dtype)
    return pl.pallas_call(
        functools.partial(halo_kernel, count, half),
        out_shape=(like, like),
        in_specs=[ANY],
        out_specs=(ANY, ANY),
        scratch_shapes=[pltpu.SemaphoreType.DMA((band.shape[0],))] * 4,
        compiler_params=pltpu.CompilerParams(collective_id=0, has_side_effects=True, vmem_limit_bytes=LIMIT),
        name="density_rows",
    )(band)


def masked(values, live, stacked):
    slots, block = values.shape[1], values.shape[2]
    for k in range(slots):
        block_values = values[0, k]
        stacked[k * block : (k + 1) * block] = jnp.where(k < live, block_values, jnp.zeros_like(block_values))


def density_kernel(slots_ref, live_ref, band, below, above, values, density, projected, window, stacked, lhs, sems):
    b = pl.program_id(0)
    rows, width, block = band.shape[0], band.shape[1], band.shape[2]
    half = (width - 1) // 2
    slots = values.shape[1]
    first = lax.axis_index("space") * rows - half

    @pl.when(b == 0)
    def _():
        copies = [
            pltpu.make_async_copy(part, window.at[pl.ds(i * rows, rows)], sems.at[i])
            for i, part in enumerate((below, band, above))
        ]
        for copy in copies:
            copy.start()
        for copy in copies:
            copy.wait()

    live = live_ref[b]
    masked(values, live, stacked)
    ids = [slots_ref[k, b] - first for k in range(slots)]
    whole = stacked[...]
    for k in range(slots):
        for j in range(slots):
            lhs[k * block : (k + 1) * block, j * block : (j + 1) * block] = window[ids[k], ids[j] - ids[k] + half]
    result = mm(lhs[...], whole, NN)
    total = jnp.sum(result * whole.astype(F32), axis=0, keepdims=True)
    for k in range(slots):
        part = result[k * block : (k + 1) * block]
        projected[0, k] = jnp.where(k < live, part, jnp.zeros_like(part))
    density[pl.ds(b, 1), :] = total


def density_call(slot_ids, live, band, below, above, values):
    batches, slots, block, points = values.shape
    rows, width = band.shape[:2]
    return pl.pallas_call(
        density_kernel,
        grid=(batches,),
        out_shape=(
            jax.ShapeDtypeStruct((batches, points), F32),
            jax.ShapeDtypeStruct(values.shape, F32),
        ),
        in_specs=[SMEM, SMEM, ANY, ANY, ANY, pl.BlockSpec((1, slots, block, points), lambda b: (b, 0, 0, 0))],
        out_specs=(
            pl.BlockSpec((batches, points), lambda b: (0, 0)),
            pl.BlockSpec((1, slots, block, points), lambda b: (b, 0, 0, 0)),
        ),
        scratch_shapes=[
            pltpu.VMEM((3 * rows, width, block, block), BF16),
            pltpu.VMEM((slots * block, points), BF16),
            pltpu.VMEM((slots * block, slots * block), BF16),
            pltpu.SemaphoreType.DMA((3,)),
        ],
        compiler_params=pltpu.CompilerParams(vmem_limit_bytes=LIMIT),
        name="density",
    )(slot_ids, live, band, below, above, values)


def network_kernel(
    count, density, weights, adjacency, emb_scale, emb_shift, w_one, w_two, w_nonlocal, w_out, out,
    hidden, slope, mixed, mixed_slope, table, coarse, gathered, parts, summed, s1, r1, s2, r2,
):
    me = lax.axis_index("space")
    barrier = pltpu.get_barrier_semaphore()

    def greet(i, carry):
        pl.semaphore_signal(
            barrier, inc=1, device_id={"space": lax.rem(me + i, count)}, device_id_type=pl.DeviceIdType.MESH
        )
        return carry

    lax.fori_loop(1, count, greet, 0)
    batches, points = density.shape
    channels = w_one.shape[0]
    span = CHUNK * points
    near_count = adjacency.shape[0]
    one_t, two_t = split(w_one[...].T), split(w_two[...].T)
    lines = jnp.concatenate(
        [ref[...].reshape(1, channels) for ref in (emb_scale, emb_shift, w_out)] + [jnp.zeros((125, channels), F32)],
        axis=0,
    ).T
    scale, shift, read = lines[:, 0:1], lines[:, 1:2], lines[:, 2:3]

    def row_of(ref, i):
        return jnp.concatenate([ref[i * CHUNK + j : i * CHUNK + j + 1, :] for j in range(CHUNK)], axis=1)

    def spread(row, i):
        wide = jnp.broadcast_to(row, (PAD, span))
        place = lax.broadcasted_iota(jnp.int32, (PAD, span), 0)
        lane = lax.broadcasted_iota(jnp.int32, (PAD, span), 1)
        return jnp.where(place == lane // points + i * CHUNK, wide, 0.0)

    steps = batches // CHUNK
    total = jnp.zeros((PAD, channels), F32)
    for i in range(steps):
        at = slice(i * span, (i + 1) * span)
        row = row_of(density, i)
        embedded = jnp.tanh(scale * row + shift)
        rising = (1.0 - embedded * embedded) * scale
        pre = mm3(one_t, split(embedded), NN)
        gate = 1.0 / (1.0 + jnp.exp(-pre))
        hid = pre * gate
        hidden[:, at] = hid
        slope[:, at] = mm3(one_t, split(rising), NN) * (gate * (1.0 + pre * (1.0 - gate)))
        total = total + mm3(split(spread(row_of(weights, i) * row, i)), split(hid), NT)
    coarse[...] = total
    gathered[me] = total

    pl.semaphore_wait(barrier, count - 1)

    def send_one(i, carry):
        peer = lax.rem(me + i, count)
        pltpu.make_async_remote_copy(
            src_ref=coarse, dst_ref=gathered.at[me], send_sem=s1, recv_sem=r1,
            device_id={"space": peer}, device_id_type=pl.DeviceIdType.MESH,
        ).start()
        return carry

    lax.fori_loop(1, count, send_one, 0)

    for i in range(steps):
        at = slice(i * span, (i + 1) * span)
        mixed[:, at] = mm3(two_t, split(hidden[:, at]), NN)
        mixed_slope[:, at] = mm3(two_t, split(slope[:, at]), NN)
    long = count * PAD
    line = lax.broadcasted_iota(jnp.int32, (long, 128), 0)
    place = line & (PAD - 1)
    ids = jnp.where(place < batches, (line >> 4) * batches + place, -1)
    listed = jnp.concatenate([adjacency[...], jnp.full((near_count, 128 - batches), -2, jnp.int32)], axis=1)
    hits = jnp.zeros((long, 128), F32)
    for a in range(near_count):
        hits = hits + jnp.where(listed[a : a + 1, :] == ids, 1.0 / near_count, 0.0)
    table[...] = hits.T
    turned = hits.astype(BF16)
    far = split(w_nonlocal[...])
    far_t = split(w_nonlocal[...].T)

    both = gathered.at[pl.ds(0, count - 1)]
    pltpu.make_async_copy(both, both, r1).wait()
    near = exact(table[0:PAD, :].astype(BF16), gathered[...].reshape(long, channels), NN)
    near = jnp.concatenate([near, jnp.zeros((128 - PAD, channels), F32)], axis=0)
    offsets = mm3(far_t, split(near.T), NN)

    pulled = jnp.zeros((PAD, channels), F32)
    direct = []
    for i in range(steps):
        at = slice(i * span, (i + 1) * span)
        offset = jnp.concatenate(
            [
                jnp.broadcast_to(offsets[:, i * CHUNK + j : i * CHUNK + j + 1], (channels, points))
                for j in range(CHUNK)
            ],
            axis=1,
        )
        pre = mixed[:, at] + offset
        gate = 1.0 / (1.0 + jnp.exp(-pre))
        row_w = row_of(weights, i)
        row_wd = row_w * row_of(density, i)
        bent = gate * (1.0 + pre * (1.0 - gate)) * read
        pulled = pulled + mm3(split(spread(row_wd, i)), split(bent), NT)
        energy = jnp.sum(pre * gate * read, axis=0, keepdims=True)
        direct.append(row_w * energy + row_wd * jnp.sum(bent * mixed_slope[:, at], axis=0, keepdims=True))
    grad_near = mm3(split(pulled), far, NT)
    grad_near = jnp.concatenate([grad_near, jnp.zeros((128 - PAD, channels), F32)], axis=0)
    parts[...] = exact(turned, grad_near, NN).reshape(count, PAD, channels)
    summed[me] = parts[me]

    def send_two(i, carry):
        peer = lax.rem(me + i, count)
        pltpu.make_async_remote_copy(
            src_ref=parts.at[peer], dst_ref=summed.at[me], send_sem=s2, recv_sem=r2,
            device_id={"space": peer}, device_id_type=pl.DeviceIdType.MESH,
        ).start()
        return carry

    lax.fori_loop(1, count, send_two, 0)
    for i in range(steps):
        at = slice(i * span, (i + 1) * span)
        mixed[:, at] = hidden[:, at] + row_of(density, i) * slope[:, at]
    other = summed.at[pl.ds(0, count - 1)]
    pltpu.make_async_copy(other, other, r2).wait()
    grad_coarse = jnp.sum(summed[...], axis=0)
    grad_coarse = jnp.concatenate([grad_coarse, jnp.zeros((128 - PAD, channels), F32)], axis=0).T
    for i in range(steps):
        for j in range(CHUNK):
            b = i * CHUNK + j
            piece = mixed[:, b * points : (b + 1) * points] * grad_coarse[:, b : b + 1]
            row_w = weights[b : b + 1, :]
            value = direct[i][:, j * points : (j + 1) * points] + row_w * jnp.sum(piece, axis=0, keepdims=True)
            out[b : b + 1, :] = value * row_w
    pltpu.make_async_copy(both, both, s1).wait()
    pltpu.make_async_copy(other, other, s2).wait()


def network(density, weights, adjacency, emb_scale, emb_shift, w_one, w_two, w_nonlocal, w_out, count):
    batches, points = density.shape
    channels = w_one.shape[0]
    wide = pltpu.VMEM((channels, batches * points), F32)
    slots = pltpu.VMEM((count, PAD, channels), F32)
    return pl.pallas_call(
        functools.partial(network_kernel, count),
        out_shape=jax.ShapeDtypeStruct((batches, points), F32),
        in_specs=[VMEM] * 9,
        out_specs=VMEM,
        scratch_shapes=[wide] * 4
        + [pltpu.VMEM((128, count * PAD), F32), pltpu.VMEM((PAD, channels), F32), slots, slots, slots]
        + [pltpu.SemaphoreType.DMA] * 4,
        compiler_params=pltpu.CompilerParams(collective_id=1, has_side_effects=True, vmem_limit_bytes=LIMIT),
        name="network",
    )(density, weights, adjacency, emb_scale, emb_shift, w_one, w_two, w_nonlocal, w_out)


def terms_kernel(
    rows, slots_ref, live_ref, potential, values, grads, projected, own, below, above, force, acc, facc, stacked
):
    b = pl.program_id(0)
    slots, block = values.shape[1], values.shape[2]
    width = own.shape[1]
    half = (width - 1) // 2
    first = lax.axis_index("space") * rows - half

    @pl.when(b == 0)
    def _():
        acc[...] = jnp.zeros_like(acc)
        facc[...] = jnp.zeros_like(facc)

    live = live_ref[b]
    masked(values, live, stacked)
    ids = [slots_ref[k, b] - first for k in range(slots)]
    whole = stacked[...]
    row = potential[pl.ds(b, 1), :]
    scaled = (whole.astype(F32) * row).astype(BF16)
    for j in range(slots):
        result = mm(scaled, whole[j * block : (j + 1) * block], NT)
        for k in range(slots):
            place = ids[k] * width + ids[j] - ids[k] + half
            acc[place] += result[k * block : (k + 1) * block]
    for k in range(slots):
        carried = projected[0, k] * row
        for c in range(3):
            facc[ids[k] * 3 + c] += grads[c, 0, k].astype(F32) * carried

    @pl.when(b == pl.num_programs(0) - 1)
    def _():
        for i in range(rows):
            for o in range(half + 1):
                below[i, o] = acc[i * width + half + o].astype(BF16)
                above[i, o] = acc[(2 * rows + i) * width + o].astype(BF16)
            for o in range(width):
                own[i, o] = acc[(rows + i) * width + o]
        ones = jnp.ones((8, block), BF16)
        for r in range(3 * rows):
            for c in range(3):
                high, low = split(facc[r * 3 + c])
                force[r, :, c * block : (c + 1) * block] = -2.0 * (mm(ones, high, NT) + mm(ones, low, NT))


def terms(slot_ids, live, potential, values, grads, projected, rows, width):
    batches, slots, block, points = values.shape
    four = lambda b: (0, 0, 0, 0)
    shape = (rows, width, block, block)
    part = (rows, (width + 1) // 2, block, block)
    return pl.pallas_call(
        functools.partial(terms_kernel, rows),
        grid=(batches,),
        out_shape=(
            jax.ShapeDtypeStruct(shape, F32),
            jax.ShapeDtypeStruct(part, BF16),
            jax.ShapeDtypeStruct(part, BF16),
            jax.ShapeDtypeStruct((3 * rows, 8, 3 * block), F32),
        ),
        in_specs=[
            SMEM,
            SMEM,
            pl.BlockSpec((batches, points), lambda b: (0, 0)),
            pl.BlockSpec((1, slots, block, points), lambda b: (b, 0, 0, 0)),
            pl.BlockSpec((3, 1, slots, block, points), lambda b: (0, b, 0, 0, 0)),
            pl.BlockSpec((1, slots, block, points), lambda b: (b, 0, 0, 0)),
        ],
        out_specs=(
            pl.BlockSpec(shape, four),
            pl.BlockSpec(part, four),
            pl.BlockSpec(part, four),
            pl.BlockSpec((3 * rows, 8, 3 * block), lambda b: (0, 0, 0)),
        ),
        scratch_shapes=[
            pltpu.VMEM((3 * rows * width, block, block), F32),
            pltpu.VMEM((9 * rows, block, block), F32),
            pltpu.VMEM((slots * block, points), BF16),
        ],
        compiler_params=pltpu.CompilerParams(vmem_limit_bytes=LIMIT),
        name="terms",
    )(slot_ids, live, potential, values, grads, projected)


def return_kernel(count, half, below, above, force, from_above, from_below, force_above, force_below, *sems):
    me = lax.axis_index("space")
    greet_neighbours(me, count)
    rows = below.shape[0]
    down = [(below.at[i], from_above.at[i]) for i in range(rows)]
    up = [(above.at[i], from_below.at[i]) for i in range(rows)]
    down.append((force.at[0:rows], force_above))
    up.append((force.at[2 * rows : 3 * rows], force_below))
    swap_body(count, None, None, me, up, down, *sems)


def return_swap(below, above, force, half, count):
    like = jax.ShapeDtypeStruct(below.shape, below.dtype)
    rows = below.shape[0]
    small = jax.ShapeDtypeStruct((rows,) + force.shape[1:], force.dtype)
    return pl.pallas_call(
        functools.partial(return_kernel, count, half),
        out_shape=(like, like, small, small),
        in_specs=[ANY] * 3,
        out_specs=(ANY,) * 4,
        scratch_shapes=[pltpu.SemaphoreType.DMA((rows + 1,))] * 4,
        compiler_params=pltpu.CompilerParams(collective_id=2, has_side_effects=True, vmem_limit_bytes=LIMIT),
        name="returned_rows",
    )(below, above, force)


def final_kernel(count, own, from_above, from_below, force, force_above, force_below, atoms, out, forces):
    i = pl.program_id(0)
    me = lax.axis_index("space")
    width = own.shape[1]
    half = (width - 1) // 2
    rows = force_above.shape[0]
    block = own.shape[2]
    has_above, has_below = me < count - 1, me > 0
    for o in range(width):
        gap = abs(o - half)
        if o >= half:
            upper, seen = from_above[i, gap].astype(F32), has_above
        else:
            upper, seen = from_above[jnp.maximum(i - gap, 0), gap].astype(F32).T, has_above & (i >= gap)
        if o <= half:
            lower, known = from_below[i, o].astype(F32), has_below
        else:
            lower = from_below[jnp.minimum(i + gap, rows - 1), half - gap].astype(F32).T
            known = has_below & (i + gap < rows)
        value = own[0, o] + jnp.where(seen, upper, jnp.zeros_like(upper))
        out[0, o] = value + jnp.where(known, lower, jnp.zeros_like(lower))

    @pl.when(i == pl.num_programs(0) - 1)
    def _():
        lines = []
        for c in range(3):
            pieces = []
            for r in range(rows):
                at = slice(c * block, (c + 1) * block)
                a, b = force_above[r, 0:1, at], force_below[r, 0:1, at]
                pieces.append(
                    force[rows + r, 0:1, at]
                    + jnp.where(me < count - 1, a, jnp.zeros_like(a))
                    + jnp.where(me > 0, b, jnp.zeros_like(b))
                )
            lines.append(jnp.concatenate(pieces, axis=1))
        lines = jnp.concatenate(lines + [jnp.zeros((5, rows * block), F32)], axis=0)
        named = atoms[...]
        hot = jnp.where(lax.broadcasted_iota(jnp.int32, (128, rows * block), 0) == named, 1.0, 0.0).astype(BF16)
        first, rest = lines.astype(BF16), None
        rest = lines - first.astype(F32)
        second, third = split(rest)
        result = mm(first, hot, NT) + (mm(second, hot, NT) + mm(third, hot, NT))
        forces[...] = result[0:3, 0:ATOM_DEV]


def final(own, from_above, from_below, force, force_above, force_below, atoms, count):
    rows, width, block, _ = own.shape
    row_spec = pl.BlockSpec((1, width, block, block), lambda i: (i, 0, 0, 0))
    full = lambda a: pl.BlockSpec(a.shape, lambda i: (0,) * a.ndim)
    return pl.pallas_call(
        functools.partial(final_kernel, count),
        grid=(rows,),
        out_shape=(jax.ShapeDtypeStruct(own.shape, F32), jax.ShapeDtypeStruct((3, ATOM_DEV), F32)),
        in_specs=[row_spec] + [full(from_above), full(from_below), full(force), full(force_above), full(force_below), full(atoms)],
        out_specs=(row_spec, pl.BlockSpec((3, ATOM_DEV), lambda i: (0, 0))),
        compiler_params=pltpu.CompilerParams(vmem_limit_bytes=LIMIT),
        name="final",
    )(own, from_above, from_below, force, force_above, force_below, atoms)


def per_device(
    density_band, basis_values, basis_grad, quad_weights, significant_block_list, live_counts,
    adjacency, atom_map, emb_scale, emb_shift, w_one, w_two, w_nonlocal, w_out,
):
    rows, width = density_band.shape[:2]
    half = (width - 1) // 2
    count = lax.axis_size("space")
    slot_ids = significant_block_list.T
    below, above = halo_swap(density_band, half, count)
    density, projected = density_call(
        slot_ids, live_counts, density_band, below, above, basis_values
    )
    potential = network(
        density, quad_weights, adjacency.T, emb_scale, emb_shift, w_one, w_two, w_nonlocal, w_out, count
    )
    own, low, high, force = terms(
        slot_ids, live_counts, potential, basis_values, basis_grad, projected, rows, width
    )
    from_above, from_below, force_above, force_below = return_swap(low, high, force, half, count)
    return final(own, from_above, from_below, force, force_above, force_below, atom_map, count)


def solution(mesh):
    both = ("groups", "space")
    placed = (
        P(both, None, None, None),
        P(both, None, None, None),
        P(None, both, None, None, None),
        P(both, None),
        P(both, None),
        P(both),
        P(both, None),
        P(both, None),
    ) + (P(),) * 6
    return jax.shard_map(
        per_device,
        mesh=mesh,
        in_specs=placed,
        out_specs=(P(both, None, None, None), P(None, both)),
        check_vma=False,
    )
```

```python
import functools

import jax
import jax.numpy as jnp
from jax import lax
from jax.experimental import pallas as pl
from jax.experimental.pallas import tpu as pltpu
from jax.sharding import PartitionSpec as P

ATOM_DEV = 47
PAD = 16
CHUNK = 4
F32, BF16 = jnp.float32, jnp.bfloat16
VMEM = pl.BlockSpec(memory_space=pltpu.VMEM)
SMEM = pl.BlockSpec(memory_space=pltpu.SMEM)
ANY = pl.BlockSpec(memory_space=pl.ANY)
LIMIT = 60 * 1024 * 1024
NN = (((1,), (0,)), ((), ()))
NT = (((1,), (1,)), ((), ()))


def split(value):
    high = value.astype(BF16)
    return high, (value - high.astype(F32)).astype(BF16)


def mm(left, right, dims):
    return lax.dot_general(left, right, dims, preferred_element_type=F32)


def mm3(left, right, dims):
    return mm(left[0], right[0], dims) + (
        mm(left[0], right[1], dims) + mm(left[1], right[0], dims)
    )


def exact(left, value, dims):
    first, rest = value.astype(BF16), None
    rest = value - first.astype(F32)
    second, third = split(rest)
    return mm(left, first, dims) + (mm(left, second, dims) + mm(left, third, dims))


def greet_neighbours(me, count):
    barrier = pltpu.get_barrier_semaphore()
    for step, there in ((-1, me > 0), (1, me < count - 1)):

        @pl.when(there)
        def _():
            pl.semaphore_signal(barrier, inc=1, device_id={"space": me + step}, device_id_type=pl.DeviceIdType.MESH)

    inside = (me > 0) & (me < count - 1)

    @pl.when(inside)
    def _():
        pl.semaphore_wait(barrier, 2)

    @pl.when(jnp.logical_not(inside))
    def _():
        pl.semaphore_wait(barrier, 1)


def swap_body(count, to_up, to_down, me, pairs_up, pairs_down, send_up, recv_up, send_down, recv_down):
    def made(pairs, step, send, recv):
        return [
            pltpu.make_async_remote_copy(
                src_ref=a, dst_ref=b, send_sem=send.at[i], recv_sem=recv.at[i],
                device_id={"space": me + step}, device_id_type=pl.DeviceIdType.MESH,
            )
            for i, (a, b) in enumerate(pairs)
        ]

    has_next, has_before = me < count - 1, me > 0

    @pl.when(has_next)
    def _():
        for copy in made(pairs_up, 1, send_up, recv_up):
            copy.start()

    @pl.when(has_before)
    def _():
        for copy in made(pairs_down, -1, send_down, recv_down):
            copy.start()

    @pl.when(has_next)
    def _():
        for copy in made(pairs_up, 1, send_up, recv_up):
            copy.wait_send()
        for copy in made(pairs_down, 1, send_down, recv_down):
            copy.wait_recv()

    @pl.when(has_before)
    def _():
        for copy in made(pairs_down, -1, send_down, recv_down):
            copy.wait_send()
        for copy in made(pairs_up, -1, send_up, recv_up):
            copy.wait_recv()


def masked(values, live, stacked):
    slots, block = values.shape[1], values.shape[2]
    for k in range(slots):
        block_values = values[0, k]
        stacked[k * block : (k + 1) * block] = jnp.where(k < live, block_values, jnp.zeros_like(block_values))


def density_kernel(
    count, slots_ref, live_ref, band, values, density, projected,
    window, held, stacked, lhs, kept, loads, stores, *sems
):
    me = lax.axis_index("space")
    rows, width, block = band.shape[0], band.shape[1], band.shape[2]
    half = (width - 1) // 2
    batches, slots = values.shape[0], values.shape[1]
    first = me * rows - half
    own = pltpu.make_async_copy(band, window.at[rows : 2 * rows], loads.at[0])
    own.start()
    basis = pltpu.make_async_copy(values, held, loads.at[1])
    basis.start()
    greet_neighbours(me, count)
    up = [(band.at[i, half - i : width], window.at[i, half - i : width]) for i in range(rows)]
    down = [(band.at[i, 0 : width - 1 - i], window.at[2 * rows + i, 0 : width - 1 - i]) for i in range(rows)]
    swap_body(count, None, None, me, up, down, *sems)
    own.wait()
    basis.wait()

    def batch(b, carry):
        live = live_ref[b]
        masked(held.at[pl.ds(b, 1)], live, stacked)
        ids = [jnp.clip(slots_ref[k, b] - first, 0, 3 * rows - 1) for k in range(slots)]
        whole = stacked[...]
        for k in range(slots):
            for j in range(slots):
                offset = jnp.clip(ids[j] - ids[k] + half, 0, width - 1)
                lhs[k * block : (k + 1) * block, j * block : (j + 1) * block] = window[ids[k], offset]
        result = mm(lhs[...], whole, NN)
        density[pl.ds(b, 1), :] = jnp.sum(result * whole.astype(F32), axis=0, keepdims=True)
        for k in range(slots):
            part = result[k * block : (k + 1) * block]
            kept[b, k] = jnp.where(k < live, part, jnp.zeros_like(part))
        pltpu.make_async_copy(kept.at[b], projected.at[b], stores.at[b]).start()
        return carry

    lax.fori_loop(0, batches, batch, 0)

    def stored(b, carry):
        pltpu.make_async_copy(kept.at[b], projected.at[b], stores.at[b]).wait()
        return carry

    lax.fori_loop(0, batches, stored, 0)


def density_call(slot_ids, live, band, values, count):
    batches, slots, block, points = values.shape
    rows, width = band.shape[:2]
    return pl.pallas_call(
        functools.partial(density_kernel, count),
        out_shape=(
            jax.ShapeDtypeStruct((batches, points), F32),
            jax.ShapeDtypeStruct(values.shape, F32),
        ),
        in_specs=[SMEM, SMEM, ANY, ANY],
        out_specs=(VMEM, ANY),
        scratch_shapes=[
            pltpu.VMEM((3 * rows, width, block, block), BF16),
            pltpu.VMEM(values.shape, BF16),
            pltpu.VMEM((slots * block, points), BF16),
            pltpu.VMEM((slots * block, slots * block), BF16),
            pltpu.VMEM(values.shape, F32),
            pltpu.SemaphoreType.DMA((2,)),
            pltpu.SemaphoreType.DMA((batches,)),
        ]
        + [pltpu.SemaphoreType.DMA((rows,))] * 4,
        compiler_params=pltpu.CompilerParams(collective_id=0, has_side_effects=True, vmem_limit_bytes=LIMIT),
        name="density",
    )(slot_ids, live, band, values)


def network_kernel(
    count, density, weights, adjacency, emb_scale, emb_shift, w_one, w_two, w_nonlocal, w_out, out,
    hidden, slope, mixed, mixed_slope, table, coarse, gathered, parts, summed, s1, r1, s2, r2,
):
    me = lax.axis_index("space")
    barrier = pltpu.get_barrier_semaphore()

    def greet(i, carry):
        pl.semaphore_signal(
            barrier, inc=1, device_id={"space": lax.rem(me + i, count)}, device_id_type=pl.DeviceIdType.MESH
        )
        return carry

    lax.fori_loop(1, count, greet, 0)
    batches, points = density.shape
    channels = w_one.shape[0]
    span = CHUNK * points
    near_count = adjacency.shape[0]
    one_t, two_t = split(w_one[...].T), split(w_two[...].T)
    lines = jnp.concatenate(
        [ref[...].reshape(1, channels) for ref in (emb_scale, emb_shift, w_out)] + [jnp.zeros((125, channels), F32)],
        axis=0,
    ).T
    scale, shift, read = lines[:, 0:1], lines[:, 1:2], lines[:, 2:3]

    def row_of(ref, i):
        return jnp.concatenate([ref[i * CHUNK + j : i * CHUNK + j + 1, :] for j in range(CHUNK)], axis=1)

    def spread(row, i):
        wide = jnp.broadcast_to(row, (PAD, span))
        place = lax.broadcasted_iota(jnp.int32, (PAD, span), 0)
        lane = lax.broadcasted_iota(jnp.int32, (PAD, span), 1)
        return jnp.where(place == lane // points + i * CHUNK, wide, 0.0)

    steps = batches // CHUNK
    total = jnp.zeros((PAD, channels), F32)
    for i in range(steps):
        at = slice(i * span, (i + 1) * span)
        row = row_of(density, i)
        embedded = jnp.tanh(scale * row + shift)
        rising = (1.0 - embedded * embedded) * scale
        pre = mm3(one_t, split(embedded), NN)
        gate = 1.0 / (1.0 + jnp.exp(-pre))
        hid = pre * gate
        hidden[:, at] = hid
        slope[:, at] = mm3(one_t, split(rising), NN) * (gate * (1.0 + pre * (1.0 - gate)))
        total = total + mm3(split(spread(row_of(weights, i) * row, i)), split(hid), NT)
    coarse[...] = total
    gathered[me] = total

    pl.semaphore_wait(barrier, count - 1)

    def send_one(i, carry):
        peer = lax.rem(me + i, count)
        pltpu.make_async_remote_copy(
            src_ref=coarse, dst_ref=gathered.at[me], send_sem=s1, recv_sem=r1,
            device_id={"space": peer}, device_id_type=pl.DeviceIdType.MESH,
        ).start()
        return carry

    lax.fori_loop(1, count, send_one, 0)

    for i in range(steps):
        at = slice(i * span, (i + 1) * span)
        mixed[:, at] = mm3(two_t, split(hidden[:, at]), NN)
        mixed_slope[:, at] = mm3(two_t, split(slope[:, at]), NN)
    long = count * PAD
    line = lax.broadcasted_iota(jnp.int32, (long, 128), 0)
    place = line & (PAD - 1)
    ids = jnp.where(place < batches, (line >> 4) * batches + place, -1)
    listed = jnp.concatenate([adjacency[...], jnp.full((near_count, 128 - batches), -2, jnp.int32)], axis=1)
    hits = jnp.zeros((long, 128), F32)
    for a in range(near_count):
        hits = hits + jnp.where(listed[a : a + 1, :] == ids, 1.0 / near_count, 0.0)
    table[...] = hits.T
    turned = hits.astype(BF16)
    far = split(w_nonlocal[...])
    far_t = split(w_nonlocal[...].T)

    both = gathered.at[pl.ds(0, count - 1)]
    pltpu.make_async_copy(both, both, r1).wait()
    near = exact(table[0:PAD, :].astype(BF16), gathered[...].reshape(long, channels), NN)
    near = jnp.concatenate([near, jnp.zeros((128 - PAD, channels), F32)], axis=0)
    offsets = mm3(far_t, split(near.T), NN)

    pulled = jnp.zeros((PAD, channels), F32)
    direct = []
    for i in range(steps):
        at = slice(i * span, (i + 1) * span)
        offset = jnp.concatenate(
            [
                jnp.broadcast_to(offsets[:, i * CHUNK + j : i * CHUNK + j + 1], (channels, points))
                for j in range(CHUNK)
            ],
            axis=1,
        )
        pre = mixed[:, at] + offset
        gate = 1.0 / (1.0 + jnp.exp(-pre))
        row_w = row_of(weights, i)
        row_wd = row_w * row_of(density, i)
        bent = gate * (1.0 + pre * (1.0 - gate)) * read
        pulled = pulled + mm3(split(spread(row_wd, i)), split(bent), NT)
        energy = jnp.sum(pre * gate * read, axis=0, keepdims=True)
        direct.append(row_w * energy + row_wd * jnp.sum(bent * mixed_slope[:, at], axis=0, keepdims=True))
    grad_near = mm3(split(pulled), far, NT)
    grad_near = jnp.concatenate([grad_near, jnp.zeros((128 - PAD, channels), F32)], axis=0)
    parts[...] = exact(turned, grad_near, NN).reshape(count, PAD, channels)
    summed[me] = parts[me]

    def send_two(i, carry):
        peer = lax.rem(me + i, count)
        pltpu.make_async_remote_copy(
            src_ref=parts.at[peer], dst_ref=summed.at[me], send_sem=s2, recv_sem=r2,
            device_id={"space": peer}, device_id_type=pl.DeviceIdType.MESH,
        ).start()
        return carry

    lax.fori_loop(1, count, send_two, 0)
    for i in range(steps):
        at = slice(i * span, (i + 1) * span)
        mixed[:, at] = hidden[:, at] + row_of(density, i) * slope[:, at]
    other = summed.at[pl.ds(0, count - 1)]
    pltpu.make_async_copy(other, other, r2).wait()
    grad_coarse = jnp.sum(summed[...], axis=0)
    grad_coarse = jnp.concatenate([grad_coarse, jnp.zeros((128 - PAD, channels), F32)], axis=0).T
    for i in range(steps):
        for j in range(CHUNK):
            b = i * CHUNK + j
            piece = mixed[:, b * points : (b + 1) * points] * grad_coarse[:, b : b + 1]
            row_w = weights[b : b + 1, :]
            value = direct[i][:, j * points : (j + 1) * points] + row_w * jnp.sum(piece, axis=0, keepdims=True)
            out[b : b + 1, :] = value * row_w
    pltpu.make_async_copy(both, both, s1).wait()
    pltpu.make_async_copy(other, other, s2).wait()


def network(density, weights, adjacency, emb_scale, emb_shift, w_one, w_two, w_nonlocal, w_out, count):
    batches, points = density.shape
    channels = w_one.shape[0]
    wide = pltpu.VMEM((channels, batches * points), F32)
    slots = pltpu.VMEM((count, PAD, channels), F32)
    return pl.pallas_call(
        functools.partial(network_kernel, count),
        out_shape=jax.ShapeDtypeStruct((batches, points), F32),
        in_specs=[VMEM] * 9,
        out_specs=VMEM,
        scratch_shapes=[wide] * 4
        + [pltpu.VMEM((128, count * PAD), F32), pltpu.VMEM((PAD, channels), F32), slots, slots, slots]
        + [pltpu.SemaphoreType.DMA] * 4,
        cost_estimate=pl.CostEstimate(flops=16 * 10**9, bytes_accessed=4 * 10**6, transcendentals=10**6),
        compiler_params=pltpu.CompilerParams(collective_id=1, has_side_effects=True, vmem_limit_bytes=24 * 1024 * 1024),
        name="network",
    )(density, weights, adjacency, emb_scale, emb_shift, w_one, w_two, w_nonlocal, w_out)


def terms_kernel(
    rows, slots_ref, live_ref, potential, values, grads, projected, own, below, above, force, acc, facc, stacked
):
    b = pl.program_id(0)
    slots, block = values.shape[1], values.shape[2]
    width = own.shape[1]
    half = (width - 1) // 2
    first = lax.axis_index("space") * rows - half

    @pl.when(b == 0)
    def _():
        acc[...] = jnp.zeros_like(acc)
        facc[...] = jnp.zeros_like(facc)

    live = live_ref[b]
    masked(values, live, stacked)
    ids = [slots_ref[k, b] - first for k in range(slots)]
    whole = stacked[...]
    row = potential[pl.ds(b, 1), :]
    scaled = (whole.astype(F32) * row).astype(BF16)
    for j in range(slots):
        result = mm(scaled, whole[j * block : (j + 1) * block], NT)
        for k in range(slots):
            place = ids[k] * width + ids[j] - ids[k] + half
            acc[place] += result[k * block : (k + 1) * block]
    for k in range(slots):
        carried = projected[0, k] * row
        for c in range(3):
            facc[ids[k] * 3 + c] += grads[c, 0, k].astype(F32) * carried

    @pl.when(b == pl.num_programs(0) - 1)
    def _():
        for i in range(rows):
            for o in range(half + 1):
                below[i, o] = acc[i * width + half + o].astype(BF16)
                above[i, o] = acc[(2 * rows + i) * width + o].astype(BF16)
            for o in range(width):
                own[i, o] = acc[(rows + i) * width + o]
        ones = jnp.ones((8, block), BF16)
        for r in range(3 * rows):
            for c in range(3):
                high, low = split(facc[r * 3 + c])
                force[r, :, c * block : (c + 1) * block] = -2.0 * (mm(ones, high, NT) + mm(ones, low, NT))


def terms(slot_ids, live, potential, values, grads, projected, rows, width):
    batches, slots, block, points = values.shape
    four = lambda b: (0, 0, 0, 0)
    shape = (rows, width, block, block)
    part = (rows, (width + 1) // 2, block, block)
    return pl.pallas_call(
        functools.partial(terms_kernel, rows),
        grid=(batches,),
        out_shape=(
            jax.ShapeDtypeStruct(shape, F32),
            jax.ShapeDtypeStruct(part, BF16),
            jax.ShapeDtypeStruct(part, BF16),
            jax.ShapeDtypeStruct((3 * rows, 8, 3 * block), F32),
        ),
        in_specs=[
            SMEM,
            SMEM,
            pl.BlockSpec((batches, points), lambda b: (0, 0)),
            pl.BlockSpec((1, slots, block, points), lambda b: (b, 0, 0, 0)),
            pl.BlockSpec((3, 1, slots, block, points), lambda b: (0, b, 0, 0, 0)),
            pl.BlockSpec((1, slots, block, points), lambda b: (b, 0, 0, 0)),
        ],
        out_specs=(
            pl.BlockSpec(shape, four),
            pl.BlockSpec(part, four),
            pl.BlockSpec(part, four),
            pl.BlockSpec((3 * rows, 8, 3 * block), lambda b: (0, 0, 0)),
        ),
        scratch_shapes=[
            pltpu.VMEM((3 * rows * width, block, block), F32),
            pltpu.VMEM((9 * rows, block, block), F32),
            pltpu.VMEM((slots * block, points), BF16),
        ],
        compiler_params=pltpu.CompilerParams(vmem_limit_bytes=28 * 1024 * 1024),
        name="terms",
    )(slot_ids, live, potential, values, grads, projected)


def return_kernel(count, half, below, above, force, from_above, from_below, force_above, force_below, *sems):
    me = lax.axis_index("space")
    greet_neighbours(me, count)
    rows = below.shape[0]
    down = [(below.at[i], from_above.at[i]) for i in range(rows)]
    up = [(above.at[i], from_below.at[i]) for i in range(rows)]
    down.append((force.at[0:rows], force_above))
    up.append((force.at[2 * rows : 3 * rows], force_below))
    swap_body(count, None, None, me, up, down, *sems)


def return_swap(below, above, force, half, count):
    like = jax.ShapeDtypeStruct(below.shape, below.dtype)
    rows = below.shape[0]
    small = jax.ShapeDtypeStruct((rows,) + force.shape[1:], force.dtype)
    return pl.pallas_call(
        functools.partial(return_kernel, count, half),
        out_shape=(like, like, small, small),
        in_specs=[ANY] * 3,
        out_specs=(ANY,) * 4,
        scratch_shapes=[pltpu.SemaphoreType.DMA((rows + 1,))] * 4,
        compiler_params=pltpu.CompilerParams(collective_id=2, has_side_effects=True, vmem_limit_bytes=8 * 1024 * 1024),
        name="returned_rows",
    )(below, above, force)


def final_kernel(count, own, from_above, from_below, force, force_above, force_below, atoms, out, forces):
    i = pl.program_id(0)
    me = lax.axis_index("space")
    width = own.shape[1]
    half = (width - 1) // 2
    rows = force_above.shape[0]
    block = own.shape[2]
    has_above, has_below = me < count - 1, me > 0
    for o in range(width):
        gap = abs(o - half)
        if o >= half:
            upper, seen = from_above[i, gap].astype(F32), has_above
        else:
            upper, seen = from_above[jnp.maximum(i - gap, 0), gap].astype(F32).T, has_above & (i >= gap)
        if o <= half:
            lower, known = from_below[i, o].astype(F32), has_below
        else:
            lower = from_below[jnp.minimum(i + gap, rows - 1), half - gap].astype(F32).T
            known = has_below & (i + gap < rows)
        value = own[0, o] + jnp.where(seen, upper, jnp.zeros_like(upper))
        out[0, o] = value + jnp.where(known, lower, jnp.zeros_like(lower))

    @pl.when(i == pl.num_programs(0) - 1)
    def _():
        lines = []
        for c in range(3):
            pieces = []
            for r in range(rows):
                at = slice(c * block, (c + 1) * block)
                a, b = force_above[r, 0:1, at], force_below[r, 0:1, at]
                pieces.append(
                    force[rows + r, 0:1, at]
                    + jnp.where(me < count - 1, a, jnp.zeros_like(a))
                    + jnp.where(me > 0, b, jnp.zeros_like(b))
                )
            lines.append(jnp.concatenate(pieces, axis=1))
        lines = jnp.concatenate(lines + [jnp.zeros((5, rows * block), F32)], axis=0)
        named = atoms[...]
        hot = jnp.where(lax.broadcasted_iota(jnp.int32, (128, rows * block), 0) == named, 1.0, 0.0).astype(BF16)
        first, rest = lines.astype(BF16), None
        rest = lines - first.astype(F32)
        second, third = split(rest)
        result = mm(first, hot, NT) + (mm(second, hot, NT) + mm(third, hot, NT))
        forces[...] = result[0:3, 0:ATOM_DEV]


def final(own, from_above, from_below, force, force_above, force_below, atoms, count):
    rows, width, block, _ = own.shape
    row_spec = pl.BlockSpec((1, width, block, block), lambda i: (i, 0, 0, 0))
    full = lambda a: pl.BlockSpec(a.shape, lambda i: (0,) * a.ndim)
    return pl.pallas_call(
        functools.partial(final_kernel, count),
        grid=(rows,),
        out_shape=(jax.ShapeDtypeStruct(own.shape, F32), jax.ShapeDtypeStruct((3, ATOM_DEV), F32)),
        in_specs=[row_spec] + [full(from_above), full(from_below), full(force), full(force_above), full(force_below), full(atoms)],
        out_specs=(row_spec, pl.BlockSpec((3, ATOM_DEV), lambda i: (0, 0))),
        compiler_params=pltpu.CompilerParams(vmem_limit_bytes=16 * 1024 * 1024),
        name="final",
    )(own, from_above, from_below, force, force_above, force_below, atoms)


def per_device(
    density_band, basis_values, basis_grad, quad_weights, significant_block_list, live_counts,
    adjacency, atom_map, emb_scale, emb_shift, w_one, w_two, w_nonlocal, w_out,
):
    rows, width = density_band.shape[:2]
    half = (width - 1) // 2
    count = lax.axis_size("space")
    slot_ids = significant_block_list.T
    density, projected = density_call(slot_ids, live_counts, density_band, basis_values, count)
    potential = network(
        density, quad_weights, adjacency.T, emb_scale, emb_shift, w_one, w_two, w_nonlocal, w_out, count
    )
    own, low, high, force = terms(
        slot_ids, live_counts, potential, basis_values, basis_grad, projected, rows, width
    )
    from_above, from_below, force_above, force_below = return_swap(low, high, force, half, count)
    return final(own, from_above, from_below, force, force_above, force_below, atom_map, count)


def solution(mesh):
    both = ("groups", "space")
    placed = (
        P(both, None, None, None),
        P(both, None, None, None),
        P(None, both, None, None, None),
        P(both, None),
        P(both, None),
        P(both),
        P(both, None),
        P(both, None),
    ) + (P(),) * 6
    return jax.shard_map(
        per_device,
        mesh=mesh,
        in_specs=placed,
        out_specs=(P(both, None, None, None), P(None, both)),
        check_vma=False,
    )
```
